32 devices in a mesh: tm: 16 (over z, x, core), chan: 2 (over y).
Axes of the slice: x: 2, y: 2, z: 4, core: 2. Of those that a mesh axis runs over, the one named last changes fastest.
Arguments:
- signal: bfloat16 [8192, 256], P('tm', 'chan'), may hold values from -6 to 6
- skip_in: bfloat16 [8192, 256], P('tm', 'chan'), may hold values from -6 to 6
- tap_weight: bfloat16 [4, 2, 256, 512], replicated, may hold values from -0.25 to 0.25
- tap_bias: float32 [4, 512], replicated, may hold values from -3 to 3
- res_weight: bfloat16 [3, 256, 256], replicated, may hold values from -0.375 to 0.375
- skip_weight: bfloat16 [4, 256, 256], replicated, may hold values from -0.375 to 0.375
- head_w1: float32 [256, 256], replicated, may hold values from -0.375 to 0.375
- head_b1: float32 [256], replicated, may hold values from -3 to 3
- head_w2: float32 [256, 12], replicated, may hold values from -0.375 to 0.375
- head_second_bias: float32 [12], replicated, may hold values from -3 to 3
- event_bin: int32 [64], P('tm'), may hold values from 0 to 15
- observed: int32 [64], P('tm'), may hold values 0 or 1
- valid_len: int32 [1], replicated, may hold values from 7937 to 8192
Outputs:
- window_nll: float32 [64], P(('tm', 'chan'))
- grad_input: bfloat16 [8192, 256], P('tm', 'chan')
The draws below stay inside these ranges and needn't reach their ends.
All inputs are finite; a program needn't handle non-finite values. No bound on the sum of `observed` on one device may be relied on, other than what follows from the above.
Results may differ from the reference program's by a relative error of at most 0.022.
Values may be sent and summed in bfloat16 or wider, within the bound.
A program may use at most 64 MiB of HBM per device.

```python
import jax
import jax.numpy as jnp
from jax import lax

C = 256
HID = 256
MIX = 4
NBINS = 16
LAYERS = 4
WLEN = 128
TL = 512
TOTAL = 8192
FIRST_DILATION = 512
WINDOWS = 64


def place_ends(drawn, rng, low, top_value):
    longest = drawn.shape.index(max(drawn.shape))
    spots = []
    for shift in (0, 1):
        where = [jax.random.randint(jax.random.fold_in(rng, axis), (), 0, length) for axis, length in enumerate(drawn.shape)]
        where[longest] = (where[longest] + shift) % drawn.shape[longest]
        spots.append(tuple(where))
    return drawn.at[spots[0]].set(low).at[spots[1]].set(top_value)


def block_scale(key, shape, pieces, low, largest):
    loudness = 1.0
    for axis_at, parts in pieces:
        steps = jax.random.uniform(jax.random.fold_in(jax.random.fold_in(key, 6), axis_at), (parts,), jnp.float32, low / len(pieces), largest / len(pieces))
        loudness = loudness * jnp.repeat(jnp.exp(steps), shape[axis_at] // parts).reshape((-1,) + (1,) * (len(shape) - 1 - axis_at))
    return loudness


def bell_draw(own_key, dims, deviation, most, pieces=(), held_as=jnp.bfloat16):
    result = jax.random.normal(own_key, dims, jnp.float32) * deviation
    if len(pieces) > 0:
        result = block_scale(own_key, dims, pieces, -0.22, 0.18) * result
    return jnp.clip(result, min=-most, max=most).astype(held_as)


def setup_inputs(seed: int = 0) -> dict:
    arg_keys = jax.random.split(jax.random.key(seed), 14)
    return {
        "signal": bell_draw(arg_keys[0], (TOTAL, C), 1.0, 6.0, ((0, 16), (1, 2))),
        "skip_in": bell_draw(arg_keys[1], (TOTAL, C), 1.0, 6.0, ((0, 16), (1, 2))),
        "tap_weight": bell_draw(arg_keys[2], (LAYERS, 2, C, 2 * C), (2 * C) ** -0.5, 0.25),
        "tap_bias": bell_draw(arg_keys[3], (LAYERS, 2 * C), 0.5, 3.0, (), jnp.float32),
        "res_weight": bell_draw(arg_keys[4], (LAYERS - 1, C, C), C ** -0.5, 0.375),
        "skip_weight": bell_draw(arg_keys[5], (LAYERS, C, C), C ** -0.5, 0.375),
        "head_w1": bell_draw(arg_keys[6], (C, HID), C ** -0.5, 0.375, (), jnp.float32),
        "head_b1": bell_draw(arg_keys[7], (HID,), 0.5, 3.0, (), jnp.float32),
        "head_w2": bell_draw(arg_keys[8], (HID, 3 * MIX), HID ** -0.5, 0.375, (), jnp.float32),
        "head_second_bias": bell_draw(arg_keys[9], (3 * MIX,), 0.5, 3.0, (), jnp.float32),
        "event_bin": place_ends(jax.random.randint(arg_keys[10], (WINDOWS,), 0, NBINS), jax.random.fold_in(arg_keys[10], 1), 0, NBINS - 1).astype(jnp.int32),
        "observed": place_ends((jax.random.randint(arg_keys[11], (WINDOWS,), 0, 3) < 2).astype(jnp.int32), jax.random.fold_in(arg_keys[11], 1), 0, 1),
        "valid_len": jax.random.randint(arg_keys[12], (1,), TOTAL - TL // 2 + 1, TOTAL + 1).astype(jnp.int32),
    }


def gate_values(preact, half_width):
    filters = jnp.tanh(preact[:, :half_width])
    gates = jax.nn.sigmoid(preact[:, half_width:])
    return (filters * gates).astype(jnp.bfloat16)

def gate_grads(preact, grad_gated, half_width):
    filters = jnp.tanh(preact[:, :half_width])
    gates = jax.nn.sigmoid(preact[:, half_width:])
    grad_filter = grad_gated * gates * (1.0 - filters * filters)
    gate_gradient = grad_gated * filters * gates * (1.0 - gates)
    return jnp.concatenate([grad_filter, gate_gradient], axis=1).astype(jnp.bfloat16)

def silu_slope(values):
    sig = jax.nn.sigmoid(values)
    return sig * (1.0 + values * (1.0 - sig))

def pool_windows(activity, keep_mask, window_len):
    row_count, width = activity.shape
    sums = (activity * keep_mask[:, None]).reshape(row_count // window_len, window_len, width).sum(axis=1)
    counts = keep_mask.reshape(row_count // window_len, window_len).sum(axis=1)
    return sums / jnp.maximum(counts, 1.0)[:, None]

def window_loss(pooled, bins, flags, head_w1, head_b1, head_w2, head_second_bias):
    hidden = jax.nn.silu(jnp.dot(pooled, head_w1, precision=lax.Precision.HIGHEST) + head_b1)
    params = jnp.dot(hidden, head_w2, precision=lax.Precision.HIGHEST) + head_second_bias
    mixes = params.shape[1] // 3
    logits = 4.0 * jnp.tanh(params[:, :mixes])
    mixture_log_weight = logits - jnp.log(lax.optimization_barrier(jnp.sum(jnp.exp(logits), axis=1, keepdims=True)))
    log_scale = jnp.tanh(params[:, mixes:2 * mixes])
    log_shape = 0.5 * jnp.tanh(params[:, 2 * mixes:])
    shape_value = jnp.exp(log_shape)
    log_time = jnp.log((bins.astype(jnp.float32) + 1.0) / 8.0)[:, None]
    ratio = log_time - log_scale
    power = jnp.exp(shape_value * ratio)
    log_density = log_shape - log_scale + (shape_value - 1.0) * ratio - power
    component = jnp.where(flags[:, None] == 1, log_density, -power)
    return -jnp.log(lax.optimization_barrier(jnp.sum(jnp.exp(mixture_log_weight + component), axis=1)))

def head_grads(pooled, bins, flags, head_w1, head_b1, head_w2, head_second_bias):

    def loss_of(values):
        return window_loss(values, bins, flags, head_w1, head_b1, head_w2, head_second_bias)
    nll_values, pullback = jax.vjp(loss_of, pooled)
    return (nll_values, pullback(jnp.ones_like(nll_values))[0])

def spread_rows(grad_pool, window_len):
    window_total_count, width = grad_pool.shape
    return jnp.broadcast_to(grad_pool[:, None, :], (window_total_count, window_len, width)).reshape(window_total_count * window_len, width)

def reference(signal, skip_in, tap_weight, tap_bias, res_weight, skip_weight, head_w1, head_b1, head_w2, head_second_bias, event_bin, observed, valid_len):
    total = signal.shape[0]
    width = signal.shape[1]
    current = signal
    skip_sum = skip_in.astype(jnp.float32)
    preacts = []
    for layer_number in range(LAYERS):
        delay_span_length = FIRST_DILATION * 2 ** layer_number
        delayed = jnp.concatenate([jnp.zeros((delay_span_length, width), jnp.bfloat16), current[:total - delay_span_length]], axis=0)
        preact = jnp.dot(delayed, tap_weight[layer_number, 0], preferred_element_type=jnp.float32)
        preact = preact + jnp.dot(current, tap_weight[layer_number, 1], preferred_element_type=jnp.float32) + tap_bias[layer_number]
        gated = gate_values(preact, width)
        preacts.append(preact)
        if layer_number < LAYERS - 1:
            current = (current.astype(jnp.float32) + jnp.dot(gated, res_weight[layer_number], preferred_element_type=jnp.float32)).astype(jnp.bfloat16)
        skip_sum = skip_sum + jnp.dot(gated, skip_weight[layer_number], preferred_element_type=jnp.float32)
    keep_mask = (jnp.arange(total, dtype=jnp.int32) < valid_len[0]).astype(jnp.float32)
    pooled = pool_windows(jax.nn.silu(skip_sum), keep_mask, WLEN)
    nll_values, grad_pool = head_grads(pooled, event_bin, observed, head_w1, head_b1, head_w2, head_second_bias)
    grad_skip = (spread_rows(grad_pool, WLEN) * keep_mask[:, None] * silu_slope(skip_sum)).astype(jnp.bfloat16)
    grad_rows = None
    for layer_number in range(LAYERS - 1, -1, -1):
        delay_span_length = FIRST_DILATION * 2 ** layer_number
        grad_gated = jnp.dot(grad_skip, skip_weight[layer_number].T, preferred_element_type=jnp.float32)
        if grad_rows is not None:
            grad_gated = grad_gated + jnp.dot(grad_rows, res_weight[layer_number].T, preferred_element_type=jnp.float32)
        preactivation_gradient = gate_grads(preacts[layer_number], grad_gated, width)
        ahead = jnp.concatenate([preactivation_gradient[delay_span_length:], jnp.zeros((delay_span_length, 2 * width), jnp.bfloat16)], axis=0)
        summed = jnp.dot(preactivation_gradient, tap_weight[layer_number, 1].T, preferred_element_type=jnp.float32)
        summed = summed + jnp.dot(ahead, tap_weight[layer_number, 0].T, preferred_element_type=jnp.float32)
        if grad_rows is not None:
            summed = summed + grad_rows.astype(jnp.float32)
        grad_rows = summed.astype(jnp.bfloat16)
    return (nll_values, grad_rows)
```

```python
import functools

import jax
import jax.numpy as jnp
from jax import lax
from jax.experimental import pallas as pl
from jax.experimental.pallas import tpu as pltpu
from jax.sharding import PartitionSpec as P

WLEN = 128
MESH = pl.DeviceIdType.MESH
F32 = jnp.float32
BF16 = jnp.bfloat16
X_PART, SKIP_PART, OLD_SAME, OLD_CROSS, X_NEXT, B_BACK, B0_SAME, B0_CROSS, A_CROSS = 0, 1, 2, 3, 4, 7, 10, 11, 12
ITEMS = 13


def mm(a, b):
    return jnp.dot(a, b, preferred_element_type=F32)


def mm_t(a, b, precision=None):
    return lax.dot_general(a, b, (((1,), (1,)), ((), ())), precision=precision, preferred_element_type=F32)


def sigmoid(v):
    return 0.5 * jnp.tanh(0.5 * v) + 0.5


def head(pooled, bin_at, flag, w1, b1, w2, b2):
    best = lax.Precision.HIGHEST
    pre = jnp.dot(pooled, w1, precision=best, preferred_element_type=F32) + b1
    sig = jax.nn.sigmoid(pre)
    hidden = pre * sig
    mixes = w2.shape[1] // 3
    parts = [w2[:, i * mixes : (i + 1) * mixes] for i in range(3)]
    p_l, p_s, p_k = (
        jnp.dot(hidden, parts[i], precision=best, preferred_element_type=F32) + b2[:, i * mixes : (i + 1) * mixes]
        for i in range(3)
    )
    tan_l, log_scale, tan_k = jnp.tanh(p_l), jnp.tanh(p_s), jnp.tanh(p_k)
    logits, log_shape = 4.0 * tan_l, 0.5 * tan_k
    log_pi = logits - jnp.log(jnp.sum(jnp.exp(logits), axis=1, keepdims=True))
    shape_value = jnp.exp(log_shape)
    log_time = jnp.log(jnp.full(p_l.shape, (bin_at.astype(F32) + 1.0) / 8.0, F32))
    seen = jnp.full(p_l.shape, flag, jnp.int32) == 1
    seen_one = jnp.where(seen, 1.0, 0.0)
    ratio = log_time - log_scale
    power = jnp.exp(shape_value * ratio)
    density = log_shape - log_scale + (shape_value - 1.0) * ratio - power
    terms = jnp.exp(log_pi + jnp.where(seen, density, -power))
    total = jnp.sum(terms, axis=1, keepdims=True)
    nll = -jnp.log(total)
    share = terms / total
    d_l = (jnp.exp(log_pi) - share) * 4.0 * (1.0 - tan_l * tan_l)
    d_s = -share * shape_value * (power - seen_one) * (1.0 - log_scale * log_scale)
    d_k = -share * (seen_one + shape_value * ratio * (seen_one - power)) * 0.5 * (1.0 - tan_k * tan_k)
    d_hidden = mm_t(d_l, parts[0], best) + mm_t(d_s, parts[1], best) + mm_t(d_k, parts[2], best)
    d_pre = d_hidden * sig * (1.0 + pre * (1.0 - sig))
    return nll, mm_t(d_pre, w1, best)


def kernel(
    n, layers, windows,
    signal, skip_in, tap, bias, res, skw, w1, b1, w2, b2, bins, flags, limit,
    nll_ref, out_ref,
    xin, skin, old0, xs, olds, tan_f, sig_a, skips, bsend, brecv, b0send, b0recv, a_own, a_send, a_recv, send_sem, recv_sem,
):
    me, c = lax.axis_index("tm"), lax.axis_index("chan")
    other = 1 - c
    half = windows * WLEN
    part = signal.shape[1]
    shifts = [n // 16 * 2**k for k in range(layers)]

    barrier = pltpu.get_barrier_semaphore()
    expected = jnp.int32(1)
    pl.semaphore_signal(barrier, inc=1, device_id=(me, other), device_id_type=MESH)
    for k, shift in enumerate(shifts):
        for target, ok in ((me + shift, me + shift < n), (me - shift, me >= shift)):
            lanes = (c, other) if k == 0 else (c,)
            for lane in lanes:

                @pl.when(ok)
                def _(target=target, lane=lane):
                    pl.semaphore_signal(barrier, inc=1, device_id=(target, lane), device_id_type=MESH)

            expected = expected + jnp.where(ok, len(lanes), 0).astype(jnp.int32)
    pl.semaphore_wait(barrier, expected)

    def copy(src, dst, item, j, tm_to, lane):
        return pltpu.make_async_remote_copy(
            src_ref=src, dst_ref=dst, send_sem=send_sem.at[item, j], recv_sem=recv_sem.at[item, j],
            device_id=(tm_to, lane), device_id_type=MESH,
        )

    sends = []

    def send(cond, *args):
        sends.append((cond, args))
        if cond is None:
            copy(*args).start()
        else:

            @pl.when(cond)
            def _():
                copy(*args).start()

    def await_in(cond, dst, item, j):
        def wait():
            copy(dst, dst, item, j, me, other).wait_recv()

        if cond is None:
            wait()
        else:
            pl.when(cond)(wait)

    def later(k):
        return me + shifts[k] < n

    def earlier(k):
        return me >= shifts[k]

    def own_rows(j):
        return pl.ds(pl.multiple_of(c * half + j * WLEN, WLEN), WLEN)

    def other_rows(j):
        return pl.ds(pl.multiple_of(other * half + j * WLEN, WLEN), WLEN)

    chunks = range(windows)
    for j in chunks:
        send(None, signal.at[other_rows(j), :], xin.at[c, j], X_PART, j, me, other)
        send(later(0), signal.at[own_rows(j), :], old0.at[c, j], OLD_SAME, j, me + shifts[0], c)
        send(later(0), signal.at[other_rows(j), :], old0.at[c, j], OLD_CROSS, j, me + shifts[0], other)
    for j in chunks:
        send(None, skip_in.at[other_rows(j), :], skin.at[c, j], SKIP_PART, j, me, other)

    for j in chunks:
        xin[c, j] = signal[own_rows(j), :]
        skin[c, j] = skip_in[own_rows(j), :]

    @pl.when(me < shifts[0])
    def _():
        old0[...] = jnp.zeros_like(old0)

    @pl.when(me + shifts[0] >= n)
    def _():
        b0recv[...] = jnp.zeros_like(b0recv)

    for k in range(1, layers):

        @pl.when(me < shifts[k])
        def _(k=k):
            olds[k - 1] = jnp.zeros(olds.shape[1:], BF16)

        @pl.when(me + shifts[k] >= n)
        def _(k=k):
            brecv[k - 1] = jnp.zeros(brecv.shape[1:], BF16)

    width = part * 2
    fresh = {}
    for j in chunks:
        await_in(None, xin.at[other, j], X_PART, j)
        x = jnp.concatenate([xin[0, j], xin[1, j]], axis=1)
        fresh[j] = (x, mm(x, tap[0, 1]) + bias[0:1, :])

    def forward(k, j):
        x, pre = fresh[j]
        if k == 0:
            await_in(earlier(0), old0.at[c, j], OLD_SAME, j)
            await_in(earlier(0), old0.at[other, j], OLD_CROSS, j)
            old = jnp.concatenate([old0[0, j], old0[1, j]], axis=1)
        else:
            await_in(earlier(k), olds.at[k - 1, j], X_NEXT + k - 1, j)
            old = olds[k - 1, j]
        pre = pre + mm(old, tap[k, 0])
        fil, gate = jnp.tanh(pre[:, :width]), sigmoid(pre[:, width:])
        z = (fil * gate).astype(BF16)
        if k < layers - 1:
            x = (x.astype(F32) + mm(z, res[k])).astype(BF16)
            xs[k, j] = x
            send(later(k + 1), xs.at[k, j], olds.at[k, j], X_NEXT + k, j, me + shifts[k + 1], c)
        tan_f[k, j] = fil
        sig_a[k, j] = gate
        if k == 0:
            await_in(None, skin.at[other, j], SKIP_PART, j)
            base = jnp.concatenate([skin[0, j], skin[1, j]], axis=1).astype(F32)
        else:
            base = skips[j]
        skips[j] = base + mm(z, skw[k])
        if k < layers - 1:
            fresh[j] = (x, mm(x, tap[k + 1, 1]) + bias[k + 1 : k + 2, :])

    for k in range(layers):
        for j in chunks:
            forward(k, j)

    grads = {}
    own_terms = {}

    def loss(j):
        s = skips[j]
        first = me * 2 * half + c * half + j * WLEN
        rows = first + lax.broadcasted_iota(jnp.int32, (WLEN, 1), 0)
        last = limit[0]
        keep = jnp.where(rows < last, 1.0, 0.0)
        sig = sigmoid(s)
        count = jnp.clip(last - first, 0, WLEN).astype(F32)
        pooled = jnp.sum(s * sig * keep, axis=0, keepdims=True) / jnp.maximum(count, 1.0)
        at = c * windows + j
        nll, grad = head(
            jnp.broadcast_to(pooled, (8, width)), bins[at], flags[at], w1[...], b1[...], w2[...], b2[...]
        )
        nll_ref[j : j + 1, :] = jnp.broadcast_to(nll[0:1, :], (1, nll_ref.shape[1]))
        grads[j] = (grad[0:1, :] * keep * (sig * (1.0 + s * (1.0 - sig)))).astype(BF16)

    def backward(k, j):
        if k == layers - 1:
            loss(j)
        grad_z = mm_t(grads[j], skw[k])
        above = None
        if k < layers - 1:
            await_in(later(k + 1), brecv.at[k, j], B_BACK + k, j)
            above = (own_terms[j] + brecv[k, j].astype(F32)).astype(BF16)
            grad_z = grad_z + mm_t(above, res[k])
        fil, gate = tan_f[k, j], sig_a[k, j]
        through = grad_z * gate
        grad_pre = jnp.concatenate(
            [through * (1.0 - fil * fil), through * fil * (1.0 - gate)], axis=1
        ).astype(BF16)
        back = mm_t(grad_pre, tap[k, 0]).astype(BF16)
        if k > 0:
            bsend[k - 1, j] = back
            send(earlier(k), bsend.at[k - 1, j], brecv.at[k - 1, j], B_BACK + k - 1, j, me - shifts[k], c)
        else:
            b0send[0, j] = back[:, :part]
            b0send[1, j] = back[:, part:]
            send(earlier(0), b0send.at[c, j], b0recv.at[c, j], B0_SAME, j, me - shifts[0], c)
            send(earlier(0), b0send.at[other, j], b0recv.at[c, j], B0_CROSS, j, me - shifts[0], other)
        own = mm_t(grad_pre, tap[k, 1])
        if above is not None:
            own = own + above.astype(F32)
        if k > 0:
            own_terms[j] = own
        else:
            a_own[0, j], a_own[1, j] = own[:, :part], own[:, part:]
            low = own.astype(BF16)
            a_send[0, j], a_send[1, j] = low[:, :part], low[:, part:]
            send(None, a_send.at[other, j], a_recv.at[j], A_CROSS, j, me, other)

    for k in range(layers - 1, -1, -1):
        for j in chunks:
            backward(k, j)

    for j in chunks:
        await_in(later(0), b0recv.at[c, j], B0_SAME, j)
        out_ref[own_rows(j), :] = (a_own[c, j] + b0recv[c, j].astype(F32)).astype(BF16)
        await_in(None, a_recv.at[j], A_CROSS, j)
        await_in(later(0), b0recv.at[other, j], B0_CROSS, j)
        out_ref[other_rows(j), :] = (a_recv[j].astype(F32) + b0recv[other, j].astype(F32)).astype(BF16)

    for cond, args in sends:
        if cond is None:
            copy(*args).wait_send()
        else:

            @pl.when(cond)
            def _(args=args):
                copy(*args).wait_send()


def local(
    signal, skip_in, tap_weight, tap_bias, res_weight, skip_weight,
    head_w1, head_b1, head_w2, head_second_bias, event_bin, observed, valid_len,
):
    n = lax.axis_size("tm")
    layers = tap_weight.shape[0]
    rows, part = signal.shape
    windows = rows // WLEN // 2
    width = 2 * part
    vmem = pl.BlockSpec(memory_space=pltpu.VMEM)
    smem = pl.BlockSpec(memory_space=pltpu.SMEM)
    flops = 2 * windows * WLEN * width * width * (6 * layers + 6 * layers)
    nll, grad = pl.pallas_call(
        functools.partial(kernel, n, layers, windows),
        out_shape=(
            jax.ShapeDtypeStruct((windows, 128), F32),
            jax.ShapeDtypeStruct((rows, part), BF16),
        ),
        in_specs=[vmem] * 10 + [smem] * 3,
        out_specs=(vmem, vmem),
        scratch_shapes=[
            pltpu.VMEM((2, windows, WLEN, part), BF16),
            pltpu.VMEM((2, windows, WLEN, part), BF16),
            pltpu.VMEM((2, windows, WLEN, part), BF16),
            pltpu.VMEM((layers - 1, windows, WLEN, width), BF16),
            pltpu.VMEM((layers - 1, windows, WLEN, width), BF16),
            pltpu.VMEM((layers, windows, WLEN, width), F32),
            pltpu.VMEM((layers, windows, WLEN, width), F32),
            pltpu.VMEM((windows, WLEN, width), F32),
            pltpu.VMEM((layers - 1, windows, WLEN, width), BF16),
            pltpu.VMEM((layers - 1, windows, WLEN, width), BF16),
            pltpu.VMEM((2, windows, WLEN, part), BF16),
            pltpu.VMEM((2, windows, WLEN, part), BF16),
            pltpu.VMEM((2, windows, WLEN, part), F32),
            pltpu.VMEM((2, windows, WLEN, part), BF16),
            pltpu.VMEM((windows, WLEN, part), BF16),
            pltpu.SemaphoreType.DMA((ITEMS, windows)),
            pltpu.SemaphoreType.DMA((ITEMS, windows)),
        ],
        compiler_params=pltpu.CompilerParams(
            collective_id=0, has_side_effects=True, vmem_limit_bytes=40 * 1024 * 1024
        ),
        cost_estimate=pl.CostEstimate(flops=flops, bytes_accessed=4 * 1024 * 1024, transcendentals=0),
    )(
        signal, skip_in, tap_weight, tap_bias, res_weight, skip_weight,
        head_w1, head_b1[None, :], head_w2, head_second_bias[None, :], event_bin, observed, valid_len,
    )
    return nll[:, 0], grad


def solution(mesh):
    return jax.shard_map(
        local,
        mesh=mesh,
        in_specs=(
            P("tm", "chan"), P("tm", "chan"), P(), P(), P(), P(), P(), P(), P(), P(), P("tm"), P("tm"), P(),
        ),
        out_specs=(P(("tm", "chan")), P("tm", "chan")),
        check_vma=False,
    )
```

```python
import functools

import jax
import jax.numpy as jnp
from jax import lax
from jax.experimental import pallas as pl
from jax.experimental.pallas import tpu as pltpu
from jax.sharding import PartitionSpec as P

WLEN = 128
MESH = pl.DeviceIdType.MESH
F32 = jnp.float32
BF16 = jnp.bfloat16
X_PART, SKIP_PART, OLD_SAME, OLD_CROSS, X_NEXT, B_BACK, B0_SAME, B0_CROSS, A_CROSS = 0, 1, 2, 3, 4, 7, 10, 11, 12
ITEMS = 13


def mm(a, b):
    return jnp.dot(a, b, preferred_element_type=F32)


def mm_t(a, b, precision=None):
    return lax.dot_general(a, b, (((1,), (1,)), ((), ())), precision=precision, preferred_element_type=F32)


def sigmoid(v):
    return 0.5 * jnp.tanh(0.5 * v) + 0.5


def split3(v):
    high = v.astype(BF16)
    rest = v - high.astype(F32)
    mid = rest.astype(BF16)
    return high, mid, (rest - mid.astype(F32)).astype(BF16)


def row_product(row, parts, product):
    high, mid, low = (v.astype(F32) for v in split3(row))
    at = lax.broadcasted_iota(jnp.int32, (8, row.shape[1]), 0)
    stack = jnp.where(at == 0, high, jnp.where(at == 1, mid, jnp.where(at == 2, low, 0.0))).astype(BF16)
    total = product(stack, parts[2]) + product(stack, parts[1]) + product(stack, parts[0])
    return jnp.sum(total, axis=0, keepdims=True)


def head(pooled, bin_at, flag, w1_parts, b1, w2, b2):
    pre = row_product(pooled, w1_parts, mm) + b1
    sig = sigmoid(pre)
    hidden = pre * sig
    p_l, p_s, p_k = (jnp.sum(w2[i] * hidden, axis=1, keepdims=True) + b2[i] for i in range(3))
    tan_l, log_scale, tan_k = jnp.tanh(p_l), jnp.tanh(p_s), jnp.tanh(p_k)
    logits, log_shape = 4.0 * tan_l, 0.5 * tan_k
    log_pi = logits - jnp.log(jnp.sum(jnp.exp(logits), axis=0, keepdims=True))
    shape_value = jnp.exp(log_shape)
    log_time = jnp.log(jnp.full(p_l.shape, (bin_at.astype(F32) + 1.0) / 8.0, F32))
    seen = jnp.full(p_l.shape, flag, jnp.int32) == 1
    seen_one = jnp.where(seen, 1.0, 0.0)
    ratio = log_time - log_scale
    power = jnp.exp(shape_value * ratio)
    density = log_shape - log_scale + (shape_value - 1.0) * ratio - power
    terms = jnp.exp(log_pi + jnp.where(seen, density, -power))
    total = jnp.sum(terms, axis=0, keepdims=True)
    nll = -jnp.log(total)
    share = terms / total
    d_l = (jnp.exp(log_pi) - share) * 4.0 * (1.0 - tan_l * tan_l)
    d_s = -share * shape_value * (power - seen_one) * (1.0 - log_scale * log_scale)
    d_k = -share * (seen_one + shape_value * ratio * (seen_one - power)) * 0.5 * (1.0 - tan_k * tan_k)
    d_hidden = jnp.sum(d_l * w2[0] + d_s * w2[1] + d_k * w2[2], axis=0, keepdims=True)
    d_pre = d_hidden * sig * (1.0 + pre * (1.0 - sig))
    return nll, row_product(d_pre, w1_parts, mm_t)


def kernel(
    n, layers, windows,
    signal, skip_in, tap_far, bias, res_far, skw_far, w1_far, b1, w2, b2, bins, flags, limit,
    nll_ref, out_ref,
    xin, skin, old0, xs, olds, tan_f, sig_a, skips, bsend, brecv, b0send, b0recv, a_own, a_send, a_recv, tap, res, skw, w1, w1_split, load_sem, send_sem, recv_sem,
):
    me, c = lax.axis_index("tm"), lax.axis_index("chan")
    other = 1 - c
    half = windows * WLEN
    part = signal.shape[1]
    shifts = [n // 16 * 2**k for k in range(layers)]

    load_at = 0

    def load(src, dst):
        nonlocal load_at
        this = pltpu.make_async_copy(src, dst, load_sem.at[load_at])
        this.start()
        load_at += 1
        return this

    mine = pl.ds(pl.multiple_of(c * half, half), half)
    load_x = load(signal.at[mine, :], xin.at[c])
    load_tap = [load(tap_far.at[0], tap.at[0])]
    load_res, load_skw = load(res_far, res), load(skw_far, skw)
    load_skip = load(skip_in.at[mine, :], skin.at[c])
    load_tap += [load(tap_far.at[k], tap.at[k]) for k in range(1, layers)]
    load_w1 = load(w1_far, w1)

    barrier = pltpu.get_barrier_semaphore()
    expected = jnp.int32(1)
    pl.semaphore_signal(barrier, inc=1, device_id=(me, other), device_id_type=MESH)
    for k, shift in enumerate(shifts):
        for target, ok in ((me + shift, me + shift < n), (me - shift, me >= shift)):
            lanes = (c, other) if k == 0 else (c,)
            for lane in lanes:

                @pl.when(ok)
                def _(target=target, lane=lane):
                    pl.semaphore_signal(barrier, inc=1, device_id=(target, lane), device_id_type=MESH)

            expected = expected + jnp.where(ok, len(lanes), 0).astype(jnp.int32)
    pl.semaphore_wait(barrier, expected)

    def copy(src, dst, item, j, tm_to, lane):
        return pltpu.make_async_remote_copy(
            src_ref=src, dst_ref=dst, send_sem=send_sem.at[item, j], recv_sem=recv_sem.at[item, j],
            device_id=(tm_to, lane), device_id_type=MESH,
        )

    sends = []

    def send(cond, *args):
        sends.append((cond, args))
        if cond is None:
            copy(*args).start()
        else:

            @pl.when(cond)
            def _():
                copy(*args).start()

    def await_in(cond, dst, item, j):
        def wait():
            copy(dst, dst, item, j, me, other).wait_recv()

        if cond is None:
            wait()
        else:
            pl.when(cond)(wait)

    def later(k):
        return me + shifts[k] < n

    def earlier(k):
        return me >= shifts[k]

    def own_rows(j):
        return pl.ds(pl.multiple_of(c * half + j * WLEN, WLEN), WLEN)

    def other_rows(j):
        return pl.ds(pl.multiple_of(other * half + j * WLEN, WLEN), WLEN)

    def spot(j):
        return pl.ds(j * WLEN, WLEN)

    chunks = range(windows)
    for j in chunks:
        send(None, signal.at[other_rows(j), :], xin.at[c, spot(j), :], X_PART, j, me, other)
        send(later(0), signal.at[own_rows(j), :], old0.at[c, j], OLD_SAME, j, me + shifts[0], c)
        send(later(0), signal.at[other_rows(j), :], old0.at[c, j], OLD_CROSS, j, me + shifts[0], other)
    for j in chunks:
        send(None, skip_in.at[other_rows(j), :], skin.at[c, spot(j), :], SKIP_PART, j, me, other)

    @pl.when(me < shifts[0])
    def _():
        old0[...] = jnp.zeros_like(old0)

    @pl.when(me + shifts[0] >= n)
    def _():
        b0recv[...] = jnp.zeros_like(b0recv)

    for k in range(1, layers):

        @pl.when(me < shifts[k])
        def _(k=k):
            olds[k - 1] = jnp.zeros(olds.shape[1:], BF16)

        @pl.when(me + shifts[k] >= n)
        def _(k=k):
            brecv[k - 1] = jnp.zeros(brecv.shape[1:], BF16)

    width = part * 2
    fresh = {}
    load_x.wait()
    load_tap[0].wait()
    for j in chunks:
        await_in(None, xin.at[other, spot(j), :], X_PART, j)
        x = jnp.concatenate([xin[0, spot(j), :], xin[1, spot(j), :]], axis=1)
        fresh[j] = (x, mm(x, tap[0, 1]) + bias[0:1, :])

    def forward(k, j):
        x, pre = fresh[j]
        if k == 0:
            await_in(earlier(0), old0.at[c, j], OLD_SAME, j)
            await_in(earlier(0), old0.at[other, j], OLD_CROSS, j)
            old = jnp.concatenate([old0[0, j], old0[1, j]], axis=1)
        else:
            await_in(earlier(k), olds.at[k - 1, j], X_NEXT + k - 1, j)
            old = olds[k - 1, j]
        pre = pre + mm(old, tap[k, 0])
        fil, gate = jnp.tanh(pre[:, :width]), sigmoid(pre[:, width:])
        z = (fil * gate).astype(BF16)
        if k < layers - 1:
            x = (x.astype(F32) + mm(z, res[k])).astype(BF16)
            xs[k, j] = x
            send(later(k + 1), xs.at[k, j], olds.at[k, j], X_NEXT + k, j, me + shifts[k + 1], c)
        tan_f[k, j] = fil
        sig_a[k, j] = gate
        if k == 0:
            await_in(None, skin.at[other, spot(j), :], SKIP_PART, j)
            base = jnp.concatenate([skin[0, spot(j), :], skin[1, spot(j), :]], axis=1).astype(F32)
        else:
            base = skips[j]
        skips[j] = base + mm(z, skw[k])
        if k < layers - 1:
            fresh[j] = (x, mm(x, tap[k + 1, 1]) + bias[k + 1 : k + 2, :])

    load_res.wait()
    load_skw.wait()
    load_skip.wait()
    for k in range(layers):
        if k + 1 < layers:
            load_tap[k + 1].wait()
        for j in chunks:
            forward(k, j)
        if k == 0:
            load_w1.wait()
            for i, piece in enumerate(split3(w1[...])):
                w1_split[i] = piece
    mixes = w2.shape[0] // 3
    w2_parts = [w2[i * mixes : (i + 1) * mixes, :] for i in range(3)]
    lane = lax.broadcasted_iota(jnp.int32, (mixes, 3 * mixes), 1)
    row = lax.broadcasted_iota(jnp.int32, (mixes, 3 * mixes), 0)
    b2_parts = [
        jnp.sum(jnp.where(lane == row + i * mixes, b2[...], 0.0), axis=1, keepdims=True) for i in range(3)
    ]

    grads = {}
    own_terms = {}

    def loss(j):
        s = skips[j]
        first = me * 2 * half + c * half + j * WLEN
        rows = first + lax.broadcasted_iota(jnp.int32, (WLEN, 1), 0)
        last = limit[0]
        keep = jnp.where(rows < last, 1.0, 0.0)
        sig = sigmoid(s)
        count = jnp.clip(last - first, 0, WLEN).astype(F32)
        pooled = jnp.sum(s * sig * keep, axis=0, keepdims=True) / jnp.maximum(count, 1.0)
        at = c * windows + j
        nll, grad = head(
            pooled, bins[at], flags[at], [w1_split[i] for i in range(3)], b1[...], w2_parts, b2_parts
        )
        nll_ref[j : j + 1, :] = jnp.broadcast_to(nll, (1, nll_ref.shape[1]))
        grads[j] = (grad * keep * (sig * (1.0 + s * (1.0 - sig)))).astype(BF16)

    def backward(k, j):
        if k == layers - 1:
            loss(j)
        grad_z = mm_t(grads[j], skw[k])
        above = None
        if k < layers - 1:
            await_in(later(k + 1), brecv.at[k, j], B_BACK + k, j)
            above = (own_terms[j] + brecv[k, j].astype(F32)).astype(BF16)
            grad_z = grad_z + mm_t(above, res[k])
        fil, gate = tan_f[k, j], sig_a[k, j]
        through = grad_z * gate
        grad_pre = jnp.concatenate(
            [through * (1.0 - fil * fil), through * fil * (1.0 - gate)], axis=1
        ).astype(BF16)
        back = mm_t(grad_pre, tap[k, 0]).astype(BF16)
        if k > 0:
            bsend[k - 1, j] = back
            send(earlier(k), bsend.at[k - 1, j], brecv.at[k - 1, j], B_BACK + k - 1, j, me - shifts[k], c)
        else:
            b0send[0, j] = back[:, :part]
            b0send[1, j] = back[:, part:]
            send(earlier(0), b0send.at[c, j], b0recv.at[c, j], B0_SAME, j, me - shifts[0], c)
            send(earlier(0), b0send.at[other, j], b0recv.at[c, j], B0_CROSS, j, me - shifts[0], other)
        own = mm_t(grad_pre, tap[k, 1])
        if above is not None:
            own = own + above.astype(F32)
        if k > 0:
            own_terms[j] = own
        else:
            a_own[0, j], a_own[1, j] = own[:, :part], own[:, part:]
            low = own.astype(BF16)
            a_send[0, j], a_send[1, j] = low[:, :part], low[:, part:]
            send(None, a_send.at[other, j], a_recv.at[j], A_CROSS, j, me, other)

    for k in range(layers - 1, -1, -1):
        for j in chunks:
            backward(k, j)

    for j in chunks:
        await_in(later(0), b0recv.at[c, j], B0_SAME, j)
        out_ref[own_rows(j), :] = (a_own[c, j] + b0recv[c, j].astype(F32)).astype(BF16)
        await_in(None, a_recv.at[j], A_CROSS, j)
        await_in(later(0), b0recv.at[other, j], B0_CROSS, j)
        out_ref[other_rows(j), :] = (a_recv[j].astype(F32) + b0recv[other, j].astype(F32)).astype(BF16)

    for cond, args in sends:
        if cond is None:
            copy(*args).wait_send()
        else:

            @pl.when(cond)
            def _(args=args):
                copy(*args).wait_send()


def local(
    signal, skip_in, tap_weight, tap_bias, res_weight, skip_weight,
    head_w1, head_b1, head_w2, head_second_bias, event_bin, observed, valid_len,
):
    n = lax.axis_size("tm")
    layers = tap_weight.shape[0]
    rows, part = signal.shape
    windows = rows // WLEN // 2
    width = 2 * part
    vmem = pl.BlockSpec(memory_space=pltpu.VMEM)
    far = pl.BlockSpec(memory_space=pltpu.HBM)
    smem = pl.BlockSpec(memory_space=pltpu.SMEM)
    flops = 2 * windows * WLEN * width * width * (6 * layers + 6 * layers)
    nll, grad = pl.pallas_call(
        functools.partial(kernel, n, layers, windows),
        out_shape=(
            jax.ShapeDtypeStruct((windows, 128), F32),
            jax.ShapeDtypeStruct((rows, part), BF16),
        ),
        in_specs=[far, far, far, vmem, far, far, far, vmem, vmem, vmem, smem, smem, smem],
        out_specs=(vmem, vmem),
        scratch_shapes=[
            pltpu.VMEM((2, windows * WLEN, part), BF16),
            pltpu.VMEM((2, windows * WLEN, part), BF16),
            pltpu.VMEM((2, windows, WLEN, part), BF16),
            pltpu.VMEM((layers - 1, windows, WLEN, width), BF16),
            pltpu.VMEM((layers - 1, windows, WLEN, width), BF16),
            pltpu.VMEM((layers, windows, WLEN, width), F32),
            pltpu.VMEM((layers, windows, WLEN, width), F32),
            pltpu.VMEM((windows, WLEN, width), F32),
            pltpu.VMEM((layers - 1, windows, WLEN, width), BF16),
            pltpu.VMEM((layers - 1, windows, WLEN, width), BF16),
            pltpu.VMEM((2, windows, WLEN, part), BF16),
            pltpu.VMEM((2, windows, WLEN, part), BF16),
            pltpu.VMEM((2, windows, WLEN, part), F32),
            pltpu.VMEM((2, windows, WLEN, part), BF16),
            pltpu.VMEM((windows, WLEN, part), BF16),
            pltpu.VMEM(tap_weight.shape, BF16),
            pltpu.VMEM(res_weight.shape, BF16),
            pltpu.VMEM(skip_weight.shape, BF16),
            pltpu.VMEM(head_w1.shape, F32),
            pltpu.VMEM((3, *head_w1.shape), BF16),
            pltpu.SemaphoreType.DMA((layers + 5,)),
            pltpu.SemaphoreType.DMA((ITEMS, windows)),
            pltpu.SemaphoreType.DMA((ITEMS, windows)),
        ],
        compiler_params=pltpu.CompilerParams(
            collective_id=0, has_side_effects=True, vmem_limit_bytes=60 * 1024 * 1024
        ),
        cost_estimate=pl.CostEstimate(flops=flops, bytes_accessed=4 * 1024 * 1024, transcendentals=0),
    )(
        signal, skip_in, tap_weight, tap_bias, res_weight, skip_weight,
        head_w1, head_b1[None, :], head_w2.T, head_second_bias[None, :], event_bin, observed, valid_len,
    )
    return nll[:, 0], grad


def solution(mesh):
    return jax.shard_map(
        local,
        mesh=mesh,
        in_specs=(
            P("tm", "chan"), P("tm", "chan"), P(), P(), P(), P(), P(), P(), P(), P(), P("tm"), P("tm"), P(),
        ),
        out_specs=(P(("tm", "chan")), P("tm", "chan")),
        check_vma=False,
    )
```
